32 devices in a mesh: section: 2 (over core), tensor: 2 (over x), dp: 8 (over z, y).
Axes of the slice: x: 2, y: 2, z: 4, core: 2. Of those that a mesh axis runs over, the one named last changes fastest.
Arguments:
- inputs: bfloat16 [16, 1024, 768], P('dp', 'tensor'), may hold values from -6 to 6
- segments: int32 [16, 1024], P('dp'), may hold values from 0 to 3, never falling along the last dimension, each value on 1 to 768 neighbouring positions
- cotangent: bfloat16 [16, 1024, 768], P('dp', 'tensor'), may hold values from -6 to 6
- norm_gains: bfloat16 [2, 2, 768], P('section'), may hold values from 0.5 to 1.5
- shared_biases: bfloat16 [2, 4, 768], P('section'), may hold values from -1.5 to 1.5
- w_qkv: bfloat16 [2, 768, 3, 768], P('section', None, None, 'tensor'), may hold values from -0.3125 to 0.3125
- qv_bias: bfloat16 [2, 2, 768], P('section', None, 'tensor'), may hold values from -1.5 to 1.5
- w_out: bfloat16 [2, 768, 768], P('section', 'tensor'), may hold values from -0.875 to 0.875
- w_up: bfloat16 [2, 768, 3072], P('section', None, 'tensor'), may hold values from -0.21875 to 0.21875
- up_bias: bfloat16 [2, 3072], P('section', 'tensor'), may hold values from -1.5 to 1.5
- w_down: bfloat16 [2, 3072, 768], P('section', 'tensor'), may hold values from -0.109375 to 0.109375
Outputs:
- activations: bfloat16 [2, 16, 1024, 768], P('section', 'dp', 'tensor')
- input_grads: bfloat16 [2, 16, 1024, 768], P('section', 'dp', 'tensor')
- grad_qkv: float32 [2, 768, 3, 768], P('section', None, None, 'tensor')
- grad_qv_bias: float32 [2, 2, 768], P('section', None, 'tensor')
- grad_out: float32 [2, 768, 768], P('section', 'tensor')
- grad_up: float32 [2, 768, 3072], P('section', None, 'tensor')
- grad_up_bias: float32 [2, 3072], P('section', 'tensor')
- grad_down: float32 [2, 3072, 768], P('section', 'tensor')
- grad_gains: float32 [2, 2, 768], P('section')
- grad_shifts: float32 [2, 4, 768], P('section')
The draws below stay inside these ranges and needn't reach their ends.
Inputs may be any that keep to these rules, and one draw needn't show every extreme that they name: `segments`: each row's numbers never fall; a number's run is 1 to 768 tokens long, and one run of every row has exactly that length.
All inputs are finite; a program needn't handle non-finite values.
Results may differ from the reference program's by a relative error of at most 0.03.
Values may be sent and summed in bfloat16 or wider, within the bound.
A program may use at most 320 MiB of HBM per device.

```python
import math
import jax
import jax.numpy as jnp
import numpy as np
from jax import lax

D = 768
FF = 3072
HEAD = 64
SEQ = 1024
SEQS = 16


def steps_of(stream_key, shape, pieces, smallest, largest):
    def one(axis_at, parts):
        draws = jax.random.uniform(jax.random.fold_in(jax.random.fold_in(stream_key, 6), axis_at), (parts,), jnp.float32, smallest / len(pieces), largest / len(pieces))
        return jnp.repeat(jnp.exp(draws), shape[axis_at] // parts).reshape((-1,) + (1,) * (len(shape) - axis_at - 1))

    factor_of = one(*pieces[0])
    for cut in pieces[1:]:
        factor_of = factor_of * one(*cut)
    return factor_of


def split_up(count, total, most, lean):
    weights = [(1 << 20) // math.isqrt(grade ** lean) + 1 for grade in range(2, count + 1)]
    rest, given = total - most - (count - 1), [1] * (count - 1)
    while rest > 0:
        free = [i for i in range(count - 1) if given[i] < most]
        pool, budget = sum([weights[i] for i in free]), rest
        for i in free:
            addition = min(most - given[i], max(1, budget * weights[i] // pool), rest)
            given[i] = given[i] + addition
            rest = rest - addition
    return np.array([most] + given)


def ragged_sizes(rng, number_of, total, bound, lean):
    if number_of == 2:
        one = jax.random.randint(rng, (), max(1, total - bound), min(bound, total - 1) + 1)
        return jnp.stack([one, total - one])
    sizes = jnp.asarray(split_up(number_of, total, bound, lean), jnp.int32)
    couples = (number_of - 1) // 2
    giver, taker = sizes[1:1 + 2 * couples:2], sizes[2:2 + 2 * couples:2]
    margin = jnp.minimum(giver - 1, bound - taker)
    passed = jax.random.randint(jax.random.fold_in(rng, 1), (couples,), 0, 1 << 20) % (margin + 1)
    sizes = sizes.at[1:1 + 2 * couples:2].set(giver - passed).at[2:2 + 2 * couples:2].set(taker + passed)
    return sizes[jax.random.permutation(jax.random.fold_in(rng, 2), number_of)]


def scatter_about(key, shape, deviation, reach, shards=(), kind=jnp.bfloat16):
    result = deviation * jax.random.normal(key, shape, jnp.float32)
    if shards:
        result = result * steps_of(key, shape, shards, -0.22, 0.18)
    return jnp.clip(result, -reach, reach).astype(kind)


def setup_inputs(seed: int = 0) -> dict:
    arg_keys = jax.random.split(jax.random.key(seed), 12)
    return {
        "inputs": scatter_about(arg_keys[0], (SEQS, SEQ, D), 1.0, 6.0, ((0, 8), (1, 2))),
        "segments": jax.vmap(lambda own: jnp.searchsorted(jnp.cumsum(ragged_sizes(own, 4, SEQ, 3 * SEQ // 4, 1)), jnp.arange(SEQ), side="right"))(jax.random.split(arg_keys[1], SEQS)).reshape((SEQS, SEQ)).astype(jnp.int32),
        "cotangent": scatter_about(arg_keys[2], (SEQS, SEQ, D), 1.0, 6.0, ((0, 8), (1, 2))),
        "norm_gains": jnp.clip(1.0 + 0.1 * jax.random.normal(arg_keys[3], (2, 2, D), jnp.float32), 0.5, 1.5).astype(jnp.bfloat16),
        "shared_biases": scatter_about(arg_keys[4], (2, 4, D), 0.3, 1.5, ((0, 2),)),
        "w_qkv": scatter_about(arg_keys[5], (2, D, 3, D), (D // 2) ** -0.5, 0.3125, ((0, 2), (3, 2))),
        "qv_bias": scatter_about(arg_keys[6], (2, 2, D), 0.3, 1.5, ((0, 2), (2, 2))),
        "w_out": scatter_about(arg_keys[7], (2, D, D), (D // 16) ** -0.5, 0.875, ((0, 2), (1, 2))),
        "w_up": scatter_about(arg_keys[8], (2, D, FF), D ** -0.5, 0.21875, ((0, 2), (2, 2))),
        "up_bias": scatter_about(arg_keys[9], (2, FF), 0.3, 1.5, ((0, 2), (1, 2))),
        "w_down": scatter_about(arg_keys[10], (2, FF, D), FF ** -0.5, 0.109375, ((0, 2), (1, 2))),
    }


@jax.custom_vjp
def low(v):
    return lax.optimization_barrier(v.astype(jnp.bfloat16)).astype(jnp.float32)

@jax.custom_vjp
def low_back(v):
    return v

def low_keep(v):
    return (low(v), None)

def low_pass(kept, grad):
    return (grad,)

def back_keep(v):
    return (v, None)

def back_low(kept, grad):
    return (low(grad),)
low.defvjp(low_keep, low_pass)
low_back.defvjp(back_keep, back_low)
HIGH = lax.Precision.HIGHEST
eps_norm = 1e-05

def norm_rows(values_in, gain, shift):
    row_mean = lax.optimization_barrier(jnp.mean(values_in, axis=-1, keepdims=True))
    centred = values_in - row_mean
    variance = lax.optimization_barrier(jnp.mean(centred * centred, axis=-1, keepdims=True))
    return centred * lax.rsqrt(variance + eps_norm) * gain + shift

def attend_block(query_block, begin_at, key_rows, value_rows, seg_ids):
    block_len = query_block.shape[0]
    scores = jnp.einsum('qhd,khd->hqk', query_block, key_rows, precision=HIGH)
    scores = low_back(scores)
    q_pos = begin_at + jnp.arange(block_len, dtype=jnp.int32)
    k_pos = jnp.arange(key_rows.shape[0], dtype=jnp.int32)
    q_seg = lax.dynamic_slice_in_dim(seg_ids, begin_at, block_len)
    allowed = (k_pos[None, :] <= q_pos[:, None]) & (q_seg[:, None] == seg_ids[None, :])
    scores = jnp.where(allowed[None], scores, -1e+30)
    row_top = lax.optimization_barrier(jnp.max(scores, axis=-1, keepdims=True))
    weights = jnp.exp(scores - row_top)
    prob_rows = low(weights / lax.optimization_barrier(jnp.sum(weights, axis=-1, keepdims=True)))
    return jnp.einsum('hqk,khd->qhd', prob_rows, value_rows, precision=HIGH)

def attend(queries, key_rows, value_rows, seg_ids):
    seq_total = queries.shape[0]
    block_count = max(1, seq_total // 512)
    block_len = seq_total // block_count
    query_blocks = queries.reshape(block_count, block_len, queries.shape[1], queries.shape[2])
    begins = jnp.arange(block_count, dtype=jnp.int32) * block_len

    def per_block(block_item):
        return attend_block(block_item[0], block_item[1], key_rows, value_rows, seg_ids)
    mixed_rows = lax.map(jax.checkpoint(per_block), (query_blocks, begins))
    return mixed_rows.reshape(queries.shape)

def one_layer(layer_in, seg_ids, params):
    gain_rows, shifts, w_qkv, qv_bias, w_out, w_up, up_bias, w_down = params
    seq_total = layer_in.shape[0]
    head_count = D // HEAD
    normed = low(norm_rows(layer_in, gain_rows[0], shifts[0]))
    projected = jnp.dot(normed, w_qkv.reshape(D, 3 * D), precision=HIGH).reshape(seq_total, 3, D)
    queries = low(low_back(projected[:, 0] + qv_bias[0]) * HEAD ** (-0.5))
    key_rows = low(low_back(projected[:, 1]))
    value_rows = low(low_back(projected[:, 2] + qv_bias[1]))
    mixed_rows = attend(queries.reshape(seq_total, head_count, HEAD), key_rows.reshape(seq_total, head_count, HEAD), value_rows.reshape(seq_total, head_count, HEAD), seg_ids)
    mixed_rows = low(low_back(mixed_rows.reshape(seq_total, D)))
    branch = low_back(jnp.dot(mixed_rows, w_out, precision=HIGH) + shifts[2])
    middle = layer_in + branch
    normed2 = low(norm_rows(middle, gain_rows[1], shifts[1]))
    hidden = low_back(jnp.dot(normed2, w_up, precision=HIGH) + up_bias)
    active = low(jax.nn.gelu(hidden, approximate=True))
    branch2 = low_back(jnp.dot(active, w_down, precision=HIGH) + shifts[3])
    return middle + branch2

def run_section(rows_all, segments, params):

    def per_seq(seq_item):
        return one_layer(seq_item[0], seq_item[1], params)
    return lax.map(jax.checkpoint(per_seq), (rows_all, segments))

def reference(inputs, segments, cotangent, norm_gains, shared_biases, w_qkv, qv_bias, w_out, w_up, up_bias, w_down):
    weight_list = (norm_gains, shared_biases, w_qkv, qv_bias, w_out, w_up, up_bias, w_down)
    first_params = tuple((param[0].astype(jnp.float32) for param in weight_list))
    second_params = tuple((param[1].astype(jnp.float32) for param in weight_list))

    def first_section(rows_all, params):
        return low_back(low(run_section(rows_all, segments, params)))

    def second_section(rows_all, params):
        return low(run_section(rows_all, segments, params))
    middle, first_back = jax.vjp(first_section, inputs.astype(jnp.float32), first_params)
    final_rows, second_back = jax.vjp(second_section, middle, second_params)
    grad_middle, second_grads = second_back(cotangent.astype(jnp.float32))
    grad_inputs, first_grads = first_back(grad_middle)
    activations = jnp.stack([middle, final_rows]).astype(jnp.bfloat16)
    input_grads = jnp.stack([grad_inputs, grad_middle]).astype(jnp.bfloat16)
    stacked = tuple((jnp.stack([left, right]) for left, right in zip(first_grads, second_grads)))
    return (activations, input_grads, stacked[2], stacked[3], stacked[4], stacked[5], stacked[6], stacked[7], stacked[0], stacked[1])
```

```python
import jax
import jax.numpy as jnp
from jax import lax
from jax.sharding import PartitionSpec as P

HEAD = 64


eps_norm = 1e-05


GROUP = ("section", "tensor")


def flip(block, axis):
    return lax.ppermute(block, axis, [(0, 1), (1, 0)])


def spread(layer, block):
    near = lax.ppermute(block, GROUP, [(layer * 2 + t, t * 2 + t) for t in range(2)])
    far = lax.ppermute(block, GROUP, [(layer * 2 + t, t * 2 + 1 - t) for t in range(2)])
    return jnp.where(lax.axis_index("section") == lax.axis_index("tensor"), near, far)


def pair_sum(partial):
    part = partial.astype(jnp.bfloat16)
    return part.astype(jnp.float32) + flip(part, "section").astype(jnp.float32)


def collect(grad):
    x = lax.axis_index("tensor")
    rows = grad.shape[0] // 2
    low = grad.astype(jnp.bfloat16)
    first, second = low[:rows], low[rows:]
    same = jnp.where(x == 0, first, second)
    other = jnp.where(x == 0, second, first)
    a = lax.ppermute(same, GROUP, [(c * 2 + x, x * 2 + c) for c in range(2) for x in range(2)])
    b = lax.ppermute(
        other, GROUP, [(c * 2 + x, (1 - x) * 2 + c) for c in range(2) for x in range(2)]
    )
    return (a.astype(jnp.float32) + b.astype(jnp.float32)).astype(jnp.bfloat16)


def whole_rows(halves):
    x = lax.axis_index("tensor")
    own = jnp.where(x == 0, halves[0], halves[1])
    away = flip(jnp.where(x == 0, halves[1], halves[0]), "tensor")
    return jnp.concatenate([jnp.where(x == 0, own, away), jnp.where(x == 0, away, own)], axis=0)


def placed_rows(of_layers):
    s, x = lax.axis_index("section"), lax.axis_index("tensor")
    rows = jnp.where(s == 0, of_layers[0], of_layers[1])
    half = rows.shape[0] // 2
    first, second = rows[:half], rows[half:]
    keep = jnp.where(x == 0, first, second)
    away = flip(jnp.where(x == 0, second, first), "tensor")
    return jnp.stack([jnp.where(x == 0, keep, away), jnp.where(x == 0, away, keep)])[None]


def smooth(values_in):
    return jax.nn.gelu(values_in, approximate=True)


def dot_rows(left, right):
    return lax.dot_general(
        left, right, (((0,), (0,)), ((), ())), preferred_element_type=jnp.float32
    )


def dot_last(left, right):
    return lax.dot_general(
        left, right, (((1,), (1,)), ((), ())), preferred_element_type=jnp.float32
    )


def norm_forward(rows_in, gain, shift):
    row_mean = jnp.mean(rows_in, axis=-1, keepdims=True)
    centred = rows_in - row_mean
    inv_dev = lax.rsqrt(jnp.mean(centred * centred, axis=-1, keepdims=True) + eps_norm)
    unit_rows = centred * inv_dev
    return (unit_rows * gain + shift, unit_rows, inv_dev)


def norm_backward(grad_out, unit_rows, inv_dev, gain):
    scaled = grad_out * gain
    grad_in = inv_dev * (
        scaled
        - jnp.mean(scaled, axis=-1, keepdims=True)
        - unit_rows * jnp.mean(scaled * unit_rows, axis=-1, keepdims=True)
    )
    return (grad_in, jnp.sum(grad_out * unit_rows, axis=0), jnp.sum(grad_out, axis=0))


def block_shape(seq_total):
    block_count = max(1, seq_total // 512)
    return (block_count, seq_total // block_count)


def allowed_block(begin_at, block_len, seg_ids):
    q_pos = begin_at + jnp.arange(block_len)
    k_pos = jnp.arange(seg_ids.shape[0])
    q_seg = seg_ids[begin_at : begin_at + block_len]
    return (k_pos[None, :] <= q_pos[:, None]) & (q_seg[:, None] == seg_ids[None, :])


def attention_forward(queries, key_rows, value_rows, seg_ids):
    block_count, block_len = block_shape(queries.shape[0])
    pieces, totals = ([], [])
    for block_no in range(block_count):
        begin_at = block_no * block_len
        scores = jnp.einsum(
            "qhd,khd->hqk",
            queries[begin_at : begin_at + block_len],
            key_rows,
            preferred_element_type=jnp.float32,
        )
        scores = jnp.where(allowed_block(begin_at, block_len, seg_ids)[None], scores, -1e30)
        row_top = jnp.max(scores, axis=-1, keepdims=True)
        weights = jnp.exp(scores - row_top)
        summed = jnp.sum(weights, axis=-1, keepdims=True)
        prob_rows = (weights / summed).astype(jnp.bfloat16)
        pieces.append(
            jnp.einsum("hqk,khd->qhd", prob_rows, value_rows, preferred_element_type=jnp.float32)
        )
        totals.append(row_top + jnp.log(summed))
    return (jnp.concatenate(pieces, axis=0), jnp.concatenate(totals, axis=1))


def attention_backward(queries, key_rows, value_rows, seg_ids, totals, grad_mixed):
    block_count, block_len = block_shape(queries.shape[0])
    grad_queries = []
    grad_keys = jnp.zeros(key_rows.shape, jnp.float32)
    grad_values = jnp.zeros(value_rows.shape, jnp.float32)
    for block_no in range(block_count):
        begin_at = block_no * block_len
        part_query = queries[begin_at : begin_at + block_len]
        part_grad = grad_mixed[begin_at : begin_at + block_len]
        scores = jnp.einsum(
            "qhd,khd->hqk", part_query, key_rows, preferred_element_type=jnp.float32
        )
        scores = jnp.where(allowed_block(begin_at, block_len, seg_ids)[None], scores, -1e30)
        prob_exact = jnp.exp(scores - totals[:, begin_at : begin_at + block_len])
        prob_rows = prob_exact.astype(jnp.bfloat16)
        grad_probs = jnp.einsum(
            "qhd,khd->hqk", part_grad, value_rows, preferred_element_type=jnp.float32
        )
        row_dot = jnp.sum(prob_exact * grad_probs, axis=-1, keepdims=True)
        grad_scores = (prob_exact * (grad_probs - row_dot)).astype(jnp.bfloat16)
        grad_queries.append(
            jnp.einsum("hqk,khd->qhd", grad_scores, key_rows, preferred_element_type=jnp.float32)
        )
        grad_keys = grad_keys + jnp.einsum(
            "hqk,qhd->khd", grad_scores, part_query, preferred_element_type=jnp.float32
        )
        grad_values = grad_values + jnp.einsum(
            "hqk,qhd->khd", prob_rows, part_grad, preferred_element_type=jnp.float32
        )
    return (jnp.concatenate(grad_queries, axis=0), grad_keys, grad_values)


def layer_forward(rows_in, seg_ids, params):
    small, qkv_mat, out_mat, up_mat, down_mat = params
    gains, shifts, qv_rows, up_shift = small
    seq_total, model_width = rows_in.shape
    local_width = out_mat.shape[0]
    head_count = local_width // HEAD
    q_scale = HEAD ** (-0.5)
    rows_in = rows_in.astype(jnp.float32)
    normed, unit1, inv1 = norm_forward(rows_in, gains[0], shifts[0])
    normed = normed.astype(jnp.bfloat16)
    projected = jnp.dot(normed, qkv_mat, preferred_element_type=jnp.float32).reshape(
        seq_total, 3, local_width
    )
    queries = ((projected[:, 0] + qv_rows[0]) * q_scale).astype(jnp.bfloat16)
    key_rows = projected[:, 1].astype(jnp.bfloat16)
    value_rows = (projected[:, 2] + qv_rows[1]).astype(jnp.bfloat16)
    heads = (seq_total, head_count, HEAD)
    queries, key_rows, value_rows = (v.reshape(heads) for v in (queries, key_rows, value_rows))
    mixed, totals = attention_forward(queries, key_rows, value_rows, seg_ids)
    mixed = mixed.reshape(seq_total, local_width).astype(jnp.bfloat16)
    branch = pair_sum(jnp.dot(mixed, out_mat, preferred_element_type=jnp.float32))
    middle = rows_in + branch + shifts[2]
    normed2, unit2, inv2 = norm_forward(middle, gains[1], shifts[1])
    normed2 = normed2.astype(jnp.bfloat16)
    hidden = jnp.dot(normed2, up_mat, preferred_element_type=jnp.float32) + up_shift
    active = smooth(hidden).astype(jnp.bfloat16)
    branch2 = pair_sum(jnp.dot(active, down_mat, preferred_element_type=jnp.float32))
    output = (middle + branch2 + shifts[3]).astype(jnp.bfloat16)
    kept = (
        unit1, inv1, normed, queries, key_rows, value_rows, totals, mixed,
        unit2, inv2, normed2, hidden, active,
    )
    return (output, kept)


def layer_backward(grad_rows, seg_ids, params, kept):
    small, qkv_mat, out_mat, up_mat, down_mat = params
    gains = small[0]
    (
        unit1, inv1, normed, queries, key_rows, value_rows, totals, mixed,
        unit2, inv2, normed2, hidden, active,
    ) = kept
    seq_total = grad_rows.shape[0]
    local_width = out_mat.shape[0]
    heads = queries.shape
    q_scale = HEAD ** (-0.5)
    incoming = grad_rows.astype(jnp.float32)
    ignored, gelu_back = jax.vjp(smooth, hidden)
    grad_active = dot_last(grad_rows, down_mat)
    g_down = dot_rows(active, grad_rows)
    grad_hidden = gelu_back(grad_active)[0].astype(jnp.bfloat16)
    grad_normed2 = pair_sum(dot_last(grad_hidden, up_mat))
    g_up = dot_rows(normed2, grad_hidden)
    g_upb = jnp.sum(grad_hidden.astype(jnp.float32), axis=0)
    norm2_grad, gain2, shift2 = norm_backward(grad_normed2, unit2, inv2, gains[1])
    grad_middle = incoming + norm2_grad
    grad_branch = grad_middle.astype(jnp.bfloat16)
    grad_mixed = dot_last(grad_branch, out_mat).astype(jnp.bfloat16).reshape(heads)
    g_out = dot_rows(mixed, grad_branch)
    grad_queries, grad_keys, grad_values = attention_backward(
        queries, key_rows, value_rows, seg_ids, totals, grad_mixed
    )
    grad_queries = (grad_queries * q_scale).astype(jnp.bfloat16).reshape(seq_total, local_width)
    grad_keys = grad_keys.astype(jnp.bfloat16).reshape(seq_total, local_width)
    grad_values = grad_values.astype(jnp.bfloat16).reshape(seq_total, local_width)
    grad_proj = jnp.concatenate([grad_queries, grad_keys, grad_values], axis=1)
    grad_normed = pair_sum(dot_last(grad_proj, qkv_mat))
    g_qkv = dot_rows(normed, grad_proj)
    g_qv = jnp.stack(
        [
            jnp.sum(grad_queries.astype(jnp.float32), axis=0),
            jnp.sum(grad_values.astype(jnp.float32), axis=0),
        ]
    )
    norm1_grad, gain1, shift1 = norm_backward(grad_normed, unit1, inv1, gains[0])
    grad_in = (grad_middle + norm1_grad).astype(jnp.bfloat16)
    g_shift = jnp.stack(
        [
            shift1,
            shift2,
            jnp.sum(grad_branch.astype(jnp.float32), axis=0),
            jnp.sum(incoming, axis=0),
        ]
    )
    big = (g_qkv, g_out, g_up, g_down)
    return (grad_in, big, (g_qv, g_upb, jnp.stack([gain1, gain2]), g_shift))


def local(
    inputs,
    segments,
    cotangent,
    norm_gains,
    shared_biases,
    w_qkv,
    qv_bias,
    w_out,
    w_up,
    up_bias,
    w_down,
):
    s, x = lax.axis_index("section"), lax.axis_index("tensor")
    model_width = inputs.shape[2]
    local_width = w_qkv.shape[3]
    qkv_own = w_qkv[0].reshape(model_width, 3 * local_width)
    small_own = jnp.concatenate(
        [norm_gains[0].ravel(), shared_biases[0].ravel(), qv_bias[0].ravel(), up_bias[0].ravel()]
    )
    small_own = small_own.reshape(-1, model_width)
    rows = whole_rows(inputs)
    seg_ids = jnp.where(x == 0, segments[0], segments[1])

    def layer_params(layer):
        small = spread(layer, small_own).astype(jnp.float32)
        tail = small[6:].ravel()
        small = (
            small[:2],
            small[2:6],
            tail[: 2 * local_width].reshape(2, local_width),
            tail[2 * local_width :],
        )
        return (small,) + tuple(spread(layer, w) for w in (qkv_own, w_out[0], w_up[0], w_down[0]))

    params = [layer_params(layer) for layer in range(2)]
    outputs, kept_all = [], []
    for layer in range(2):
        rows, kept = layer_forward(rows, seg_ids, params[layer])
        outputs.append(rows)
        kept_all.append(kept)
    grad = whole_rows(cotangent)
    grads_in, bigs, smalls = [None, None], [None, None], [None, None]
    for layer in (1, 0):
        grad, big, smalls[layer] = layer_backward(grad, seg_ids, params[layer], kept_all[layer])
        grads_in[layer] = grad
        parts = tuple(collect(g) for g in big)
        if layer == 0:
            parts, bigs[1] = lax.optimization_barrier((parts, bigs[1]))
        bigs[layer] = lax.psum(parts, "dp")

    full = []
    for index in range(4):
        mine = jnp.where(s == 0, bigs[0][index], bigs[1][index])
        away = flip(jnp.where(s == 0, bigs[1][index], bigs[0][index]), "section")
        both = [jnp.where(s == 0, mine, away), jnp.where(s == 0, away, mine)]
        full.append(jnp.concatenate(both, axis=0).astype(jnp.float32))
    g_qkv, g_out, g_up, g_down = full

    packed = []
    for layer in range(2):
        g_qv, g_upb, g_gain, g_shift = smalls[layer]
        half = jnp.concatenate([g_qv.ravel(), g_upb]).reshape(-1, model_width)
        common = jnp.concatenate([g_gain, g_shift])
        packed.append(
            jnp.concatenate(
                [
                    jnp.where(s == 0, common, 0.0),
                    jnp.where(s == 0, half, 0.0),
                    jnp.where(s == 1, half, 0.0),
                ]
            )
        )
    packed = lax.psum(jnp.stack(packed), ("section", "tensor", "dp"))
    packed = jnp.where(s == 0, packed[0], packed[1])
    count = (packed.shape[0] - 6) // 2
    half = jnp.where(x == 0, packed[6 : 6 + count], packed[6 + count :]).ravel()
    return (
        placed_rows(outputs),
        placed_rows(grads_in),
        g_qkv.reshape(model_width, 3, local_width)[None],
        half[: 2 * local_width].reshape(2, local_width)[None],
        g_out[None],
        g_up[None],
        half[2 * local_width :][None],
        g_down[None],
        packed[:2][None],
        packed[2:6][None],
    )


def solution(mesh):
    return jax.shard_map(
        local,
        mesh=mesh,
        in_specs=(
            P("dp", "tensor", None),
            P("dp", None),
            P("dp", "tensor", None),
            P("section", None, None),
            P("section", None, None),
            P("section", None, None, "tensor"),
            P("section", None, "tensor"),
            P("section", "tensor", None),
            P("section", None, "tensor"),
            P("section", "tensor"),
            P("section", "tensor", None),
        ),
        out_specs=(
            P("section", "dp", "tensor", None),
            P("section", "dp", "tensor", None),
            P("section", None, None, "tensor"),
            P("section", None, "tensor"),
            P("section", "tensor", None),
            P("section", None, "tensor"),
            P("section", "tensor"),
            P("section", "tensor", None),
            P("section", None, None),
            P("section", None, None),
        ),
        check_vma=False,
    )
```

```python
import jax
import jax.numpy as jnp
from jax import lax
from jax.sharding import PartitionSpec as P

HEAD = 64


eps_norm = 1e-05


GROUP = ("section", "tensor")


def flip(block, axis):
    return lax.ppermute(block, axis, [(0, 1), (1, 0)])


def spread(layer, block):
    near = lax.ppermute(block, GROUP, [(layer * 2 + t, t * 2 + t) for t in range(2)])
    far = lax.ppermute(block, GROUP, [(layer * 2 + t, t * 2 + 1 - t) for t in range(2)])
    return jnp.where(lax.axis_index("section") == lax.axis_index("tensor"), near, far)


def pair_sum(partial):
    part = partial.astype(jnp.bfloat16)
    return part.astype(jnp.float32) + flip(part, "section").astype(jnp.float32)


def collect(grad):
    x = lax.axis_index("tensor")
    rows = grad.shape[0] // 2
    low = grad.astype(jnp.bfloat16)
    first, second = low[:rows], low[rows:]
    same = jnp.where(x == 0, first, second)
    other = jnp.where(x == 0, second, first)
    a = lax.ppermute(same, GROUP, [(c * 2 + x, x * 2 + c) for c in range(2) for x in range(2)])
    b = lax.ppermute(
        other, GROUP, [(c * 2 + x, (1 - x) * 2 + c) for c in range(2) for x in range(2)]
    )
    return (a.astype(jnp.float32) + b.astype(jnp.float32)).astype(jnp.bfloat16)


def whole_rows(halves):
    x = lax.axis_index("tensor")
    own = jnp.where(x == 0, halves[0], halves[1])
    away = flip(jnp.where(x == 0, halves[1], halves[0]), "tensor")
    return jnp.concatenate([jnp.where(x == 0, own, away), jnp.where(x == 0, away, own)], axis=0)


def placed_rows(of_layers):
    s, x = lax.axis_index("section"), lax.axis_index("tensor")
    rows = jnp.where(s == 0, of_layers[0], of_layers[1])
    half = rows.shape[0] // 2
    first, second = rows[:half], rows[half:]
    keep = jnp.where(x == 0, first, second)
    away = flip(jnp.where(x == 0, second, first), "tensor")
    return jnp.stack([jnp.where(x == 0, keep, away), jnp.where(x == 0, away, keep)])[None]


def smooth(values_in):
    return jax.nn.gelu(values_in, approximate=True)


def dot_rows(left, right):
    return lax.dot_general(
        left, right, (((0,), (0,)), ((), ())), preferred_element_type=jnp.float32
    )


def dot_last(left, right):
    return lax.dot_general(
        left, right, (((1,), (1,)), ((), ())), preferred_element_type=jnp.float32
    )


def norm_forward(rows_in, gain, shift):
    row_mean = jnp.mean(rows_in, axis=-1, keepdims=True)
    centred = rows_in - row_mean
    inv_dev = lax.rsqrt(jnp.mean(centred * centred, axis=-1, keepdims=True) + eps_norm)
    unit_rows = centred * inv_dev
    return (unit_rows * gain + shift, unit_rows, inv_dev)


def norm_backward(grad_out, unit_rows, inv_dev, gain):
    scaled = grad_out * gain
    grad_in = inv_dev * (
        scaled
        - jnp.mean(scaled, axis=-1, keepdims=True)
        - unit_rows * jnp.mean(scaled * unit_rows, axis=-1, keepdims=True)
    )
    return (grad_in, jnp.sum(grad_out * unit_rows, axis=0), jnp.sum(grad_out, axis=0))


def block_shape(seq_total):
    block_count = max(1, seq_total // 512)
    return (block_count, seq_total // block_count)


def allowed_block(begin_at, block_len, seg_ids):
    q_pos = begin_at + jnp.arange(block_len)
    k_pos = jnp.arange(seg_ids.shape[0])
    q_seg = seg_ids[begin_at : begin_at + block_len]
    return (k_pos[None, :] <= q_pos[:, None]) & (q_seg[:, None] == seg_ids[None, :])


def attention_forward(queries, key_rows, value_rows, seg_ids):
    block_count, block_len = block_shape(queries.shape[0])
    pieces, totals = ([], [])
    for block_no in range(block_count):
        begin_at = block_no * block_len
        scores = jnp.einsum(
            "qhd,khd->hqk",
            queries[begin_at : begin_at + block_len],
            key_rows,
            preferred_element_type=jnp.float32,
        )
        scores = jnp.where(allowed_block(begin_at, block_len, seg_ids)[None], scores, -1e30)
        row_top = jnp.max(scores, axis=-1, keepdims=True)
        weights = jnp.exp(scores - row_top)
        summed = jnp.sum(weights, axis=-1, keepdims=True)
        prob_rows = (weights / summed).astype(jnp.bfloat16)
        pieces.append(
            jnp.einsum("hqk,khd->qhd", prob_rows, value_rows, preferred_element_type=jnp.float32)
        )
        totals.append(row_top + jnp.log(summed))
    return (jnp.concatenate(pieces, axis=0), jnp.concatenate(totals, axis=1))


def attention_backward(queries, key_rows, value_rows, seg_ids, totals, grad_mixed):
    block_count, block_len = block_shape(queries.shape[0])
    grad_queries = []
    grad_keys = jnp.zeros(key_rows.shape, jnp.float32)
    grad_values = jnp.zeros(value_rows.shape, jnp.float32)
    for block_no in range(block_count):
        begin_at = block_no * block_len
        part_query = queries[begin_at : begin_at + block_len]
        part_grad = grad_mixed[begin_at : begin_at + block_len]
        scores = jnp.einsum(
            "qhd,khd->hqk", part_query, key_rows, preferred_element_type=jnp.float32
        )
        scores = jnp.where(allowed_block(begin_at, block_len, seg_ids)[None], scores, -1e30)
        prob_exact = jnp.exp(scores - totals[:, begin_at : begin_at + block_len])
        prob_rows = prob_exact.astype(jnp.bfloat16)
        grad_probs = jnp.einsum(
            "qhd,khd->hqk", part_grad, value_rows, preferred_element_type=jnp.float32
        )
        row_dot = jnp.sum(prob_exact * grad_probs, axis=-1, keepdims=True)
        grad_scores = (prob_exact * (grad_probs - row_dot)).astype(jnp.bfloat16)
        grad_queries.append(
            jnp.einsum("hqk,khd->qhd", grad_scores, key_rows, preferred_element_type=jnp.float32)
        )
        grad_keys = grad_keys + jnp.einsum(
            "hqk,qhd->khd", grad_scores, part_query, preferred_element_type=jnp.float32
        )
        grad_values = grad_values + jnp.einsum(
            "hqk,qhd->khd", prob_rows, part_grad, preferred_element_type=jnp.float32
        )
    return (jnp.concatenate(grad_queries, axis=0), grad_keys, grad_values)


def layer_forward(rows_in, seg_ids, params):
    small, qkv_mat, out_mat, up_mat, down_mat = params
    gains, shifts, qv_rows, up_shift = small
    seq_total, model_width = rows_in.shape
    local_width = out_mat.shape[0]
    head_count = local_width // HEAD
    q_scale = HEAD ** (-0.5)
    rows_in = rows_in.astype(jnp.float32)
    normed, unit1, inv1 = norm_forward(rows_in, gains[0], shifts[0])
    normed = normed.astype(jnp.bfloat16)
    projected = jnp.dot(normed, qkv_mat, preferred_element_type=jnp.float32).reshape(
        seq_total, 3, local_width
    )
    queries = ((projected[:, 0] + qv_rows[0]) * q_scale).astype(jnp.bfloat16)
    key_rows = projected[:, 1].astype(jnp.bfloat16)
    value_rows = (projected[:, 2] + qv_rows[1]).astype(jnp.bfloat16)
    heads = (seq_total, head_count, HEAD)
    queries, key_rows, value_rows = (v.reshape(heads) for v in (queries, key_rows, value_rows))
    mixed, totals = attention_forward(queries, key_rows, value_rows, seg_ids)
    mixed = mixed.reshape(seq_total, local_width).astype(jnp.bfloat16)
    branch = pair_sum(jnp.dot(mixed, out_mat, preferred_element_type=jnp.float32))
    middle = rows_in + branch + shifts[2]
    normed2, unit2, inv2 = norm_forward(middle, gains[1], shifts[1])
    normed2 = normed2.astype(jnp.bfloat16)
    hidden = jnp.dot(normed2, up_mat, preferred_element_type=jnp.float32) + up_shift
    active = smooth(hidden).astype(jnp.bfloat16)
    branch2 = pair_sum(jnp.dot(active, down_mat, preferred_element_type=jnp.float32))
    output = (middle + branch2 + shifts[3]).astype(jnp.bfloat16)
    kept = (
        unit1, inv1, normed, queries, key_rows, value_rows, totals, mixed,
        unit2, inv2, normed2, hidden, active,
    )
    return (output, kept)


def layer_backward(grad_rows, seg_ids, params, kept):
    small, qkv_mat, out_mat, up_mat, down_mat = params
    gains = small[0]
    (
        unit1, inv1, normed, queries, key_rows, value_rows, totals, mixed,
        unit2, inv2, normed2, hidden, active,
    ) = kept
    seq_total = grad_rows.shape[0]
    local_width = out_mat.shape[0]
    heads = queries.shape
    q_scale = HEAD ** (-0.5)
    incoming = grad_rows.astype(jnp.float32)
    ignored, gelu_back = jax.vjp(smooth, hidden)
    grad_active = dot_last(grad_rows, down_mat)
    g_down = dot_rows(active, grad_rows)
    grad_hidden = gelu_back(grad_active)[0].astype(jnp.bfloat16)
    grad_normed2 = pair_sum(dot_last(grad_hidden, up_mat))
    g_up = dot_rows(normed2, grad_hidden)
    g_upb = jnp.sum(grad_hidden.astype(jnp.float32), axis=0)
    norm2_grad, gain2, shift2 = norm_backward(grad_normed2, unit2, inv2, gains[1])
    grad_middle = incoming + norm2_grad
    grad_branch = grad_middle.astype(jnp.bfloat16)
    grad_mixed = dot_last(grad_branch, out_mat).astype(jnp.bfloat16).reshape(heads)
    g_out = dot_rows(mixed, grad_branch)
    grad_queries, grad_keys, grad_values = attention_backward(
        queries, key_rows, value_rows, seg_ids, totals, grad_mixed
    )
    grad_queries = (grad_queries * q_scale).astype(jnp.bfloat16).reshape(seq_total, local_width)
    grad_keys = grad_keys.astype(jnp.bfloat16).reshape(seq_total, local_width)
    grad_values = grad_values.astype(jnp.bfloat16).reshape(seq_total, local_width)
    grad_proj = jnp.concatenate([grad_queries, grad_keys, grad_values], axis=1)
    grad_normed = pair_sum(dot_last(grad_proj, qkv_mat))
    g_qkv = dot_rows(normed, grad_proj)
    g_qv = jnp.stack(
        [
            jnp.sum(grad_queries.astype(jnp.float32), axis=0),
            jnp.sum(grad_values.astype(jnp.float32), axis=0),
        ]
    )
    norm1_grad, gain1, shift1 = norm_backward(grad_normed, unit1, inv1, gains[0])
    grad_in = (grad_middle + norm1_grad).astype(jnp.bfloat16)
    g_shift = jnp.stack(
        [
            shift1,
            shift2,
            jnp.sum(grad_branch.astype(jnp.float32), axis=0),
            jnp.sum(incoming, axis=0),
        ]
    )
    big = (g_qkv, g_out, g_up, g_down)
    return (grad_in, big, (g_qv, g_upb, jnp.stack([gain1, gain2]), g_shift))


def local(
    inputs,
    segments,
    cotangent,
    norm_gains,
    shared_biases,
    w_qkv,
    qv_bias,
    w_out,
    w_up,
    up_bias,
    w_down,
):
    s, x = lax.axis_index("section"), lax.axis_index("tensor")
    model_width = inputs.shape[2]
    local_width = w_qkv.shape[3]
    qkv_own = w_qkv[0].reshape(model_width, 3 * local_width)
    small_own = jnp.concatenate(
        [norm_gains[0].ravel(), shared_biases[0].ravel(), qv_bias[0].ravel(), up_bias[0].ravel()]
    )
    small_own = small_own.reshape(-1, model_width)
    rows = whole_rows(inputs)
    seg_ids = jnp.where(x == 0, segments[0], segments[1])

    def layer_params(layer):
        small = spread(layer, small_own).astype(jnp.float32)
        tail = small[6:].ravel()
        small = (
            small[:2],
            small[2:6],
            tail[: 2 * local_width].reshape(2, local_width),
            tail[2 * local_width :],
        )
        return (small,) + tuple(spread(layer, w) for w in (qkv_own, w_out[0], w_up[0], w_down[0]))

    params = [layer_params(layer) for layer in range(2)]
    outputs, kept_all = [], []
    for layer in range(2):
        rows, kept = layer_forward(rows, seg_ids, params[layer])
        outputs.append(rows)
        kept_all.append(kept)
    grad = whole_rows(cotangent)
    grads_in, bigs, smalls = [None, None], [None, None], [None, None]
    for layer in (1, 0):
        grad, big, smalls[layer] = layer_backward(grad, seg_ids, params[layer], kept_all[layer])
        grads_in[layer] = grad
        parts = tuple(collect(g) for g in big)
        if layer == 0:
            parts, bigs[1] = lax.optimization_barrier((parts, bigs[1]))
            packed = jnp.stack(
                [
                    jnp.concatenate(
                        [g_gain, g_shift, jnp.concatenate([g_qv.ravel(), g_upb]).reshape(-1, model_width)]
                    )
                    for g_qv, g_upb, g_gain, g_shift in smalls
                ]
            )
            packed = (packed + flip(packed, "tensor")).astype(jnp.bfloat16)
            *parts, packed = lax.psum((*parts, packed), "dp")
            bigs[0] = tuple(parts)
        else:
            bigs[1] = lax.psum(parts, "dp")

    full = []
    for index in range(4):
        mine = jnp.where(s == 0, bigs[0][index], bigs[1][index])
        away = flip(jnp.where(s == 0, bigs[1][index], bigs[0][index]), "section")
        both = [jnp.where(s == 0, mine, away), jnp.where(s == 0, away, mine)]
        full.append(jnp.concatenate(both, axis=0).astype(jnp.float32))
    g_qkv, g_out, g_up, g_down = full

    away = flip(packed, "section")
    common = jnp.where(s == 0, packed[0, :6], packed[1, :6]).astype(jnp.float32)
    half = jnp.where(s == x, packed, away)
    half = jnp.where(s == 0, half[0, 6:], half[1, 6:]).astype(jnp.float32).ravel()
    return (
        placed_rows(outputs),
        placed_rows(grads_in),
        g_qkv.reshape(model_width, 3, local_width)[None],
        half[: 2 * local_width].reshape(2, local_width)[None],
        g_out[None],
        g_up[None],
        half[2 * local_width :][None],
        g_down[None],
        common[:2][None],
        common[2:6][None],
    )


def solution(mesh):
    return jax.shard_map(
        local,
        mesh=mesh,
        in_specs=(
            P("dp", "tensor", None),
            P("dp", None),
            P("dp", "tensor", None),
            P("section", None, None),
            P("section", None, None),
            P("section", None, None, "tensor"),
            P("section", None, "tensor"),
            P("section", "tensor", None),
            P("section", None, "tensor"),
            P("section", "tensor"),
            P("section", "tensor", None),
        ),
        out_specs=(
            P("section", "dp", "tensor", None),
            P("section", "dp", "tensor", None),
            P("section", None, None, "tensor"),
            P("section", None, "tensor"),
            P("section", "tensor", None),
            P("section", None, "tensor"),
            P("section", "tensor"),
            P("section", "tensor", None),
            P("section", None, None),
            P("section", None, None),
        ),
        check_vma=False,
    )
```
